32 devices in a mesh: wide: 8 (over z, y), tp: 4 (over x, core).
Axes of the slice: x: 2, y: 2, z: 4, core: 2. Of those that a mesh axis runs over, the one named last changes fastest.
Arguments:
- tokens: bfloat16 [16384, 768], P(('wide', 'tp')), may hold values from -6 to 6
- query_weight: bfloat16 [768, 768], P('wide', 'tp'), may hold values from -0.02734375 to 0.02734375
- key_weight: bfloat16 [768, 768], P('wide', 'tp'), may hold values from -0.21875 to 0.21875
- value_weight: bfloat16 [768, 768], P('wide', 'tp'), may hold values from -0.21875 to 0.21875
- out_weight: bfloat16 [768, 768], P('wide', 'tp'), may hold values from -1.25 to 1.25
- attn_gain: bfloat16 [768], P('wide'), may hold values from 0.5 to 1.5
- ff_gain: bfloat16 [768], P('wide'), may hold values from 0.5 to 1.5
- router: bfloat16 [768, 16], P('wide'), may hold values from -0.109375 to 0.109375
- expert_in: bfloat16 [16, 768, 3072], P('wide', None, 'tp'), may hold values from -0.21875 to 0.21875
- expert_out: bfloat16 [16, 3072, 768], P('wide', 'tp')
- bias_table: bfloat16 [12, 32], replicated, may hold values from -4 to 4
- routes: int32 [16384, 1], P(('wide', 'tp')), may hold values from 0 to 15; in each aligned block of 512 rows (0 to 511, 512 to 1023, ...) at most 40 rows name the same one
- keep: int32 [16384], P(('wide', 'tp')), may hold values 0 or 1
- cotangent: bfloat16 [16384, 768], P(('wide', 'tp')), may hold values from -6 to 6
Outputs:
- block_out: float32 [16384, 768], P(('wide', 'tp'))
- input_grad: float32 [16384, 768], P(('wide', 'tp'))
- query_grad: float32 [768, 768], P('wide', 'tp')
- key_grad: float32 [768, 768], P('wide', 'tp')
- value_grad: float32 [768, 768], P('wide', 'tp')
- out_grad: float32 [768, 768], P('wide', 'tp')
- attn_gain_grad: float32 [768], P('wide')
- ff_gain_grad: float32 [768], P('wide')
- router_grad: float32 [768, 16], P('wide')
- expert_in_grad: float32 [16, 768, 3072], P('wide', None, 'tp')
- expert_out_grad: float32 [16, 3072, 768], P('wide', 'tp')
- bias_grad: float32 [12, 32], replicated
The draws below stay inside these ranges and needn't reach their ends.
Inputs may be any that keep to these rules, and one draw needn't show every extreme that they name: `routes`: in each aligned block of 512 rows (the rows of one device) no expert is named by more than 40 rows, and one is named by exactly 40.
All inputs are finite; a program needn't handle non-finite values. No bound on the sum of `keep` on one device may be relied on, other than what follows from the above.
Results may differ from the reference program's by a relative error of at most 0.02.
Values may be sent and summed in bfloat16 or wider, within the bound.
A program may use at most 192 MiB of HBM per device.

```python
import math
import jax
import jax.numpy as jnp
import numpy as np
from jax import lax

D = 768
H = 12
HEAD = 64
FF = 3072
BUCKETS = 32
LEN = 1024
HD = 768
EXPERTS = 16
TOK_DEV = 512
TOKENS = 16384
CAP = 40


def draw_expert_out(key, part):
    key = jax.random.fold_in(key, 11)
    factor = 2.5 * EXPERTS / math.sqrt(FF)
    values = jax.random.truncated_normal(key, -4.0, 4.0, (EXPERTS, FF, D), jnp.float32)
    return (values * factor).astype(jnp.bfloat16)


def place_ends(array, key, least, high):
    index_at = [jax.random.randint(jax.random.fold_in(key, axis), (), 0, length) for axis, length in enumerate(array.shape)]
    widest = array.shape.index(max(array.shape))
    beside = index_at[:widest] + [(index_at[widest] + 1) % array.shape[widest]] + index_at[widest + 1:]
    return array.at[tuple(index_at)].set(least).at[tuple(beside)].set(high)


def levels(key, dims, pieces, least, top_value):
    level, own = 1.0, jax.random.fold_in(key, 6)
    for dim, shards_of in pieces:
        draws = jnp.exp(jax.random.uniform(jax.random.fold_in(own, dim), (shards_of,), jnp.float32, least / len(pieces), top_value / len(pieces)))
        level = level * jnp.repeat(draws, dims[dim] // shards_of).reshape([-1 if axis == dim else 1 for axis in range(len(dims))])
    return level


def routed_block(stream_key, own, number, rows, count, top, limit, slope):
    ranking = jax.random.permutation(stream_key, count)
    crowded, ordinary = shares(count, rows * top, limit, slope, True), shares(count, rows * top, limit, slope, False)
    places = jnp.arange(count)

    def named(tallies, rotation):
        used = int((tallies > 0).sum())
        fixed = max(1, used // 4)
        passed = fixed + (places - fixed + rotation * (used - fixed)) % max(1, count - fixed)
        return jnp.zeros((count,), jnp.int32).at[ranking[jnp.where(places < fixed, places, passed)]].set(jnp.asarray(tallies, jnp.int32))

    tallies = jnp.where(number % 4 == 0, named(crowded, number // 4), named(ordinary, number - number // 4 - 1))
    mixed = jax.random.permutation(jax.random.fold_in(own, 3), count)
    donor, receiver = mixed[0:count // 2 * 2:2], mixed[1:count // 2 * 2:2]
    margin = jnp.minimum(tallies[donor] - 1, limit - tallies[receiver]) // 2
    margin = jnp.where((donor == ranking[0]) | (receiver == ranking[0]) | (tallies[receiver] == 0), 0, jnp.maximum(margin, 0))
    passed = jax.random.randint(jax.random.fold_in(own, 4), (count // 2,), 0, 1 << 20) % (margin + 1)
    tallies = tallies.at[donor].add(-passed).at[receiver].add(passed)
    members = jnp.searchsorted(jnp.cumsum(tallies), jnp.arange(rows * top), side="right").astype(jnp.int32)
    table = members.reshape(top, rows).T
    table = table[jax.random.permutation(jax.random.fold_in(own, 1), rows)]
    rotation = jax.random.randint(jax.random.fold_in(own, 2), (rows, 1), 0, top)
    return jnp.take_along_axis(table, (jnp.arange(top)[None, :] + rotation) % top, axis=1)


def shares(count, total, reach, slope, full):
    loads = [(1 << 20) // math.isqrt(standing ** slope) + 1 for standing in range(1, count + 1)]
    largest = reach if full else min(reach, max(-(-total // count), total * loads[0] // sum(loads)))
    least = 1 if total - largest >= count - 1 else 0
    given, spare = [largest] + [least] * (count - 1), total - largest - least * (count - 1)
    while spare > 0:
        free = [i for i in range(1, count) if given[i] < largest] or [i for i in range(1, count) if given[i] < reach]
        whole, budget = sum([loads[i] for i in free]), spare
        for i in free:
            addition = min(reach - given[i], max(1, budget * loads[i] // whole), spare)
            given[i] = given[i] + addition
            spare = spare - addition
    return np.array(given)


def gaussian(key, shape, scale, limit, shards=(), kind=jnp.bfloat16):
    entries = scale * jax.random.normal(key, shape, jnp.float32)
    if shards:
        entries = entries * levels(key, shape, shards, -0.22, 0.18)
    return jnp.clip(entries, -limit, limit).astype(kind)


def setup_inputs(seed: int = 0) -> dict:
    key_list = jax.random.split(jax.random.key(seed), 15)
    tokens = gaussian(key_list[0], (TOKENS, D), 1.0, 6.0, ((0, 32),))
    query_weight = gaussian(key_list[1], (D, HD), (D * HEAD) ** -0.5, 0.02734375, ((0, 8), (1, 4)))
    key_weight = gaussian(key_list[2], (D, HD), D ** -0.5, 0.21875, ((0, 8), (1, 4)))
    value_weight = gaussian(key_list[3], (D, HD), D ** -0.5, 0.21875, ((0, 8), (1, 4)))
    out_weight = gaussian(key_list[4], (D, HD), (HD // 32) ** -0.5, 1.25, ((0, 8), (1, 4)))
    attn_gain = jnp.clip(1.0 + 0.1 * jax.random.normal(key_list[5], (D,), jnp.float32), 0.5, 1.5).astype(jnp.bfloat16)
    ff_gain = jnp.clip(1.0 + 0.1 * jax.random.normal(key_list[6], (D,), jnp.float32), 0.5, 1.5).astype(jnp.bfloat16)
    router = gaussian(key_list[7], (D, EXPERTS), (4 * D) ** -0.5, 0.109375, ((0, 8),))
    expert_in = gaussian(key_list[8], (EXPERTS, D, FF), D ** -0.5, 0.21875, ((0, 8), (2, 4)))
    expert_out = draw_expert_out(jax.random.fold_in(key_list[14], 71), 0)
    bias_table = gaussian(key_list[10], (H, BUCKETS), 1.0, 4.0)
    routes_keys = jax.random.split(jax.random.fold_in(key_list[11], 1), TOKENS // TOK_DEV)
    routes_turns = jax.random.permutation(jax.random.fold_in(key_list[11], 3), TOKENS // TOK_DEV)
    routes = jax.vmap(lambda own, number: routed_block(jax.random.fold_in(key_list[11], 2), own, number, TOK_DEV, EXPERTS, 1, CAP, 1))(routes_keys, routes_turns).reshape((TOKENS, 1))
    keep = place_ends((jax.random.randint(key_list[12], (TOKENS,), 0, 8) < 7).astype(jnp.int32), jax.random.fold_in(key_list[12], 1), 0, 1)
    cotangent = gaussian(key_list[13], (TOKENS, D), 1.0, 6.0, ((0, 32),))
    return dict(tokens=tokens, query_weight=query_weight, key_weight=key_weight, value_weight=value_weight, out_weight=out_weight, attn_gain=attn_gain, ff_gain=ff_gain, router=router, expert_in=expert_in, expert_out=expert_out, bias_table=bias_table, routes=routes, keep=keep, cotangent=cotangent)


@jax.custom_vjp
def low(v):
    return lax.optimization_barrier(v.astype(jnp.bfloat16)).astype(jnp.float32)

@jax.custom_vjp
def low_back(v):
    return v

def low_keep(v):
    return (low(v), None)

def low_pass(kept, grad):
    return (grad,)

def back_keep(v):
    return (v, None)

def back_low(kept, grad):
    return (low(grad),)
low.defvjp(low_keep, low_pass)
low_back.defvjp(back_keep, back_low)
epsilon = 1e-06
highest = lax.Precision.HIGHEST
bucket_bounds = [12, 16, 23, 32, 46, 64, 91]

def bucket_onehot(length, buckets):
    half = buckets // 2
    exact = half // 2
    offset = jnp.arange(-(length - 1), length, dtype=jnp.int32)
    distance = jnp.abs(offset)
    bounds = jnp.asarray(bucket_bounds, dtype=jnp.int32)
    far = exact + lax.optimization_barrier(jnp.sum((distance[:, None] >= bounds[None, :]).astype(jnp.int32), axis=1, dtype=jnp.int32))
    far = jnp.minimum(far, half - 1)
    upper = jnp.where(offset > 0, half, 0).astype(jnp.int32)
    table = upper + jnp.where(distance < exact, distance, far)
    return (table[:, None] == jnp.arange(buckets, dtype=jnp.int32)[None, :]).astype(jnp.float32)

def product(left, right):
    return jnp.dot(left, right, precision=highest)

def root_norm(value, gain):
    return value * lax.rsqrt(lax.optimization_barrier(jnp.mean(value * value, axis=-1, keepdims=True)) + epsilon) * gain

def reference(tokens, query_weight, key_weight, value_weight, out_weight, attn_gain, ff_gain, router, expert_in, expert_out, bias_table, routes, keep, cotangent):
    rows_total = tokens.shape[0]
    sequences = rows_total // LEN
    blocks_all = rows_total // TOK_DEV
    slots_all = blocks_all * CAP
    onehot_table = bucket_onehot(LEN, BUCKETS)
    positions = jnp.arange(LEN, dtype=jnp.int32)
    distance_index = positions[None, :] - positions[:, None] + (LEN - 1)
    expert_ids = routes[:, 0]
    hot = (expert_ids[:, None] == jnp.arange(EXPERTS, dtype=jnp.int32)[None, :]).astype(jnp.int32)
    per_block = hot.reshape(blocks_all, TOK_DEV, EXPERTS)
    earlier = jnp.cumsum(per_block, axis=1, dtype=jnp.int32) - per_block
    position = lax.optimization_barrier(jnp.sum(earlier * per_block, axis=2, dtype=jnp.int32)).reshape(rows_total)
    slot = jnp.arange(rows_total, dtype=jnp.int32) // TOK_DEV * CAP + position
    keep_float = keep.astype(jnp.float32)
    hot_float = hot.astype(jnp.float32)

    def forward(x_value, w_query, w_key, w_value, w_out, gain_one, gain_two, w_router, w_first_all, w_second_all, table):
        relative = product(table, onehot_table.T)
        position_bias = relative[:, distance_index]
        normed_one = low(root_norm(x_value, gain_one))

        def attend(rows):
            query = low_back(low(product(rows, w_query))).reshape(LEN, H, HEAD)
            key = low_back(low(product(rows, w_key))).reshape(LEN, H, HEAD)
            value = low_back(low(product(rows, w_value))).reshape(LEN, H, HEAD)
            scores = jnp.einsum('qhd,khd->hqk', query, key, precision=highest) + position_bias
            weights = low(jax.nn.softmax(low_back(scores), axis=-1))
            context = jnp.einsum('hqk,khd->qhd', weights, value, precision=highest)
            return low_back(low(context.reshape(LEN, H * HEAD)))
        context = lax.map(jax.checkpoint(attend), normed_one.reshape(sequences, LEN, D)).reshape(rows_total, H * HEAD)
        attended = low_back(product(context, w_out.T))
        hidden = x_value + attended
        normed_two = low(root_norm(hidden, gain_two))
        logits = low_back(product(normed_two, w_router))
        probs = jax.nn.softmax(logits, axis=-1)
        gate = lax.optimization_barrier(jnp.sum(probs * hot_float, axis=-1))
        sent = low_back(normed_two)
        buffer = jnp.zeros((EXPERTS, slots_all, D), jnp.float32).at[expert_ids, slot].set(sent)

        def expert(parts):
            rows, w_first, w_second = parts
            expert_pre = low_back(product(rows, w_first))
            expert_act = low(jax.nn.gelu(expert_pre, approximate=True))
            return low_back(low(product(expert_act, w_second)))
        results = lax.map(jax.checkpoint(expert), (buffer, w_first_all, w_second_all))
        returned = results[expert_ids, slot]
        return hidden + (keep_float * gate)[:, None] * returned
    primals = (tokens.astype(jnp.float32), query_weight.astype(jnp.float32), key_weight.astype(jnp.float32), value_weight.astype(jnp.float32), out_weight.astype(jnp.float32), attn_gain.astype(jnp.float32), ff_gain.astype(jnp.float32), router.astype(jnp.float32), expert_in.astype(jnp.float32), expert_out.astype(jnp.float32), bias_table.astype(jnp.float32))
    block_out, pullback = jax.vjp(forward, *primals)
    grads = pullback(cotangent.astype(jnp.float32))
    return (block_out, grads[0], grads[1], grads[2], grads[3], grads[4], grads[5], grads[6], grads[7], grads[8], grads[9], grads[10])
```

```python
from functools import partial

import jax
import jax.numpy as jnp
from jax import lax
from jax.experimental import pallas as pl
from jax.experimental.pallas import tpu as pltpu
from jax.sharding import PartitionSpec as P

HEAD = 64
BUCKETS = 32
LEN = 1024


epsilon = 1e-06
highest = lax.Precision.HIGHEST
bucket_bounds = [12, 16, 23, 32, 46, 64, 91]


BLOCK = 256


def bucket_onehot(length, buckets):
    half = buckets // 2
    exact = half // 2
    offset = jnp.arange(-length, length, dtype=jnp.int32)
    distance = jnp.abs(offset)
    bounds = jnp.asarray(bucket_bounds, dtype=jnp.int32)
    far = exact + jnp.sum(
        (distance[:, None] >= bounds[None, :]).astype(jnp.int32), axis=1, dtype=jnp.int32
    )
    far = jnp.minimum(far, half - 1)
    upper = jnp.where(offset > 0, half, 0).astype(jnp.int32)
    table = upper + jnp.where(distance < exact, distance, far)
    return (table[:, None] == jnp.arange(buckets, dtype=jnp.int32)[None, :]).astype(jnp.float32)


def root_norm(value, gain):
    inverse = lax.rsqrt(jnp.mean(value * value, axis=-1, keepdims=True) + epsilon)
    normed = value * inverse
    return (normed, inverse, normed * gain)


def root_norm_back(grad_in, normed, inverse, gain):
    scaled = grad_in * gain
    inner = jnp.mean(scaled * normed, axis=-1, keepdims=True)
    return (inverse * (scaled - normed * inner), jnp.sum(grad_in * normed, axis=0))


def contract_rows(left, right):
    return lax.dot_general(
        left, right, (((0,), (0,)), ((), ())), preferred_element_type=jnp.float32
    )


def contract_cols(left, right):
    return lax.dot_general(
        left, right, (((1,), (1,)), ((), ())), preferred_element_type=jnp.float32
    )


def gather_rows(rows):
    return lax.all_gather(rows, "tp", axis=0, tiled=True)


def sum_rows(term):
    return lax.psum_scatter(
        term.astype(jnp.bfloat16), "tp", scatter_dimension=0, tiled=True
    ).astype(jnp.float32)


def build_bias(heads, rel_ref, bias_ref):
    for h in range(heads):
        row = jnp.broadcast_to(rel_ref[h : h + 1, :], (BLOCK, 2 * LEN))
        bias_ref[h] = pltpu.roll(row, 0, 1, stride=1, stride_axis=0).T


def flip(value):
    return value.astype(jnp.float32).T.astype(jnp.bfloat16)


def stack_heads(parts):
    pad = jnp.zeros((BLOCK - HEAD * len(parts), parts[0].shape[1]), jnp.float32)
    return jnp.concatenate([*parts, pad], axis=0)


def head_lanes(h, value):
    lane = lax.broadcasted_iota(jnp.int32, value.shape, 1)
    return jnp.where((lane >= h * HEAD) & (lane < (h + 1) * HEAD), value, jnp.zeros_like(value))


def forward_kernel(heads, q_ref, k_ref, v_ref, rel_ref, ctx_ref, lse_ref, bias_ref, vt_ref):
    block = pl.program_id(1)

    @pl.when((pl.program_id(0) == 0) & (block == 0))
    def first():
        build_bias(heads, rel_ref, bias_ref)

    @pl.when(block == 0)
    def new_sequence():
        vt_ref[...] = flip(v_ref[...])

    start = pl.multiple_of(LEN - block * BLOCK, BLOCK)
    parts, logs = ([], [])
    for h in range(heads):
        scores = contract_cols(k_ref[...], head_lanes(h, q_ref[...]))
        scores = scores + bias_ref[h, pl.ds(start, LEN), :]
        top = jnp.max(scores, axis=0, keepdims=True)
        expo = jnp.exp(scores - top)
        total = jnp.sum(expo, axis=0, keepdims=True)
        out = jnp.dot(
            vt_ref[h * HEAD : (h + 1) * HEAD, :],
            expo.astype(jnp.bfloat16),
            preferred_element_type=jnp.float32,
        )
        parts.append(out / total)
        logs.append(top + jnp.log(total))
    ctx_ref[...] = stack_heads(parts).T.astype(jnp.bfloat16)
    logs.append(jnp.zeros((8 - heads, BLOCK), jnp.float32))
    lse_ref[0] = jnp.concatenate(logs, axis=0)


def backward_kernel(
    heads,
    q_ref,
    k_ref,
    v_ref,
    g_ref,
    lse_ref,
    rel_ref,
    dq_ref,
    dk_ref,
    dv_ref,
    drel_ref,
    bias_ref,
    kt_ref,
    sum_ref,
    dk_sum,
    dv_sum,
):
    sequence, block = (pl.program_id(0), pl.program_id(1))
    last = pl.num_programs(1) - 1

    @pl.when((sequence == 0) & (block == 0))
    def first():
        build_bias(heads, rel_ref, bias_ref)
        sum_ref[...] = jnp.zeros_like(sum_ref)

    @pl.when(block == 0)
    def new_sequence():
        kt_ref[...] = flip(k_ref[...])
        dk_sum[...] = jnp.zeros_like(dk_sum)
        dv_sum[...] = jnp.zeros_like(dv_sum)

    start = pl.multiple_of(LEN - block * BLOCK, BLOCK)
    parts = []
    for h in range(heads):
        query = head_lanes(h, q_ref[...])
        grad = head_lanes(h, g_ref[...])
        scores = contract_cols(k_ref[...], query) + bias_ref[h, pl.ds(start, LEN), :]
        weights = jnp.exp(scores - lse_ref[0, h : h + 1, :])
        grad_weights = contract_cols(v_ref[...], grad)
        inner = jnp.sum(weights * grad_weights, axis=0, keepdims=True)
        grad_scores = (weights * (grad_weights - inner)).astype(jnp.bfloat16)
        sum_ref[h, pl.ds(start, LEN), :] += grad_scores.astype(jnp.float32)
        parts.append(
            jnp.dot(
                kt_ref[h * HEAD : (h + 1) * HEAD, :],
                grad_scores,
                preferred_element_type=jnp.float32,
            )
        )
        dk_sum[...] += jnp.dot(grad_scores, query, preferred_element_type=jnp.float32)
        dv_sum[...] += jnp.dot(
            weights.astype(jnp.bfloat16), grad, preferred_element_type=jnp.float32
        )
    dq_ref[...] = stack_heads(parts).T.astype(jnp.bfloat16)

    @pl.when(block == last)
    def end_sequence():
        dk_ref[...] = dk_sum[...].astype(jnp.bfloat16)
        dv_ref[...] = dv_sum[...].astype(jnp.bfloat16)

    @pl.when((sequence == pl.num_programs(0) - 1) & (block == last))
    def end_all():
        drel_ref[...] = jnp.zeros_like(drel_ref)
        for h in range(heads):
            rows = sum_ref[h].T
            count = BLOCK
            while count > 1:
                count //= 2
                rows = rows[:count] + pltpu.roll(rows[count:], 2 * LEN - count, 1)
            drel_ref[h : h + 1, :] = rows


def attention_specs(blocks):
    query = pl.BlockSpec((BLOCK, BLOCK), lambda s, b: (s * blocks + b, 0))
    key = pl.BlockSpec((LEN, BLOCK), lambda s, b: (s, 1))
    value = pl.BlockSpec((LEN, BLOCK), lambda s, b: (s, 2))
    whole = pl.BlockSpec((LEN, BLOCK), lambda s, b: (s, 0))
    rel = pl.BlockSpec((8, 2 * LEN), lambda s, b: (0, 0))
    logs = pl.BlockSpec((1, 8, BLOCK), lambda s, b: (s * blocks + b, 0, 0))
    return (query, key, value, whole, rel, logs)


def attend(projected, relative, heads):
    rows = projected.shape[0]
    blocks = LEN // BLOCK
    query, key, value, whole, rel, logs = attention_specs(blocks)
    return pl.pallas_call(
        partial(forward_kernel, heads),
        grid=(rows // LEN, blocks),
        in_specs=[query, key, value, rel],
        out_specs=[query, logs],
        out_shape=[
            jax.ShapeDtypeStruct((rows, BLOCK), jnp.bfloat16),
            jax.ShapeDtypeStruct((rows // BLOCK, 8, BLOCK), jnp.float32),
        ],
        scratch_shapes=[
            pltpu.VMEM((heads, 2 * LEN, BLOCK), jnp.float32),
            pltpu.VMEM((BLOCK, LEN), jnp.bfloat16),
        ],
        compiler_params=pltpu.CompilerParams(vmem_limit_bytes=48 * 2**20),
        name="attend",
    )(projected, projected, projected, relative)


def attend_back(projected, grad_context, logs_in, relative, heads):
    rows = projected.shape[0]
    blocks = LEN // BLOCK
    query, key, value, whole, rel, logs = attention_specs(blocks)
    return pl.pallas_call(
        partial(backward_kernel, heads),
        grid=(rows // LEN, blocks),
        in_specs=[query, key, value, query, logs, rel],
        out_specs=[query, whole, whole, rel],
        out_shape=[
            jax.ShapeDtypeStruct((rows, BLOCK), jnp.bfloat16),
            jax.ShapeDtypeStruct((rows, BLOCK), jnp.bfloat16),
            jax.ShapeDtypeStruct((rows, BLOCK), jnp.bfloat16),
            jax.ShapeDtypeStruct((8, 2 * LEN), jnp.float32),
        ],
        scratch_shapes=[
            pltpu.VMEM((heads, 2 * LEN, BLOCK), jnp.float32),
            pltpu.VMEM((BLOCK, LEN), jnp.bfloat16),
            pltpu.VMEM((heads, 2 * LEN, BLOCK), jnp.float32),
            pltpu.VMEM((LEN, BLOCK), jnp.float32),
            pltpu.VMEM((LEN, BLOCK), jnp.float32),
        ],
        compiler_params=pltpu.CompilerParams(vmem_limit_bytes=48 * 2**20),
        name="attend_back",
    )(projected, projected, projected, grad_context, logs_in, relative)


def per_device(
    tokens,
    query_weight,
    key_weight,
    value_weight,
    out_weight,
    attn_gain,
    ff_gain,
    router,
    expert_in,
    expert_out,
    bias_table,
    routes,
    keep,
    cotangent,
):
    tp_size = lax.axis_size("tp")
    wide_size = lax.axis_size("wide")
    tok_rows, width = tokens.shape
    local_experts = expert_in.shape[0]
    experts = local_experts * wide_size
    capacity = (5 * tok_rows + 4 * experts - 1) // (4 * experts)
    head_width = query_weight.shape[1]
    local_heads = head_width // HEAD
    tokens_all = gather_rows(tokens)
    packed = jnp.concatenate(
        [
            query_weight,
            key_weight,
            value_weight,
            out_weight,
            router,
            attn_gain[:, None],
            ff_gain[:, None],
        ],
        axis=1,
    )
    packed = lax.all_gather(packed, "wide", axis=0, tiled=True)
    side = ((0, 0), (0, BLOCK - head_width))
    w_query, w_key, w_value, w_out = (
        jnp.pad(packed[:, i * head_width : (i + 1) * head_width], side) for i in range(4)
    )
    w_joint = jnp.concatenate([w_query, w_key, w_value], axis=1)
    at = 4 * head_width
    w_router = packed[:, at : at + experts]
    gain_one = packed[:, at + experts].astype(jnp.float32)
    gain_two = packed[:, at + experts + 1].astype(jnp.float32)
    onehot_table = bucket_onehot(LEN, BUCKETS)
    table_local = lax.dynamic_slice_in_dim(
        bias_table.astype(jnp.float32), lax.axis_index("tp") * local_heads, local_heads, 0
    )
    relative = jnp.pad(
        lax.dot_general(
            table_local, onehot_table, (((1,), (1,)), ((), ())), precision=highest
        ),
        ((0, 8 - local_heads), (0, 0)),
    )
    rows_one = root_norm(tokens_all.astype(jnp.float32), gain_one)[2].astype(jnp.bfloat16)
    x_value = tokens.astype(jnp.float32)
    normed_one, inverse_one, scaled_one = root_norm(x_value, gain_one)
    projected = jnp.dot(rows_one, w_joint, preferred_element_type=jnp.float32).astype(jnp.bfloat16)
    context_low, log_totals = attend(projected, relative, local_heads)
    attended = sum_rows(contract_cols(context_low, w_out))
    hidden = x_value + attended
    normed_two, inverse_two, scaled_two = root_norm(hidden, gain_two)
    rows_two = scaled_two.astype(jnp.bfloat16)
    logits = jnp.dot(rows_two, w_router, preferred_element_type=jnp.float32)
    probs = jax.nn.softmax(logits, axis=-1)
    expert_ids = routes[:, 0]
    hot = (expert_ids[:, None] == jnp.arange(experts, dtype=jnp.int32)[None, :]).astype(jnp.float32)
    gate = jnp.sum(probs * hot, axis=-1)
    lower = (jnp.arange(tok_rows)[:, None] > jnp.arange(tok_rows)[None, :]).astype(jnp.bfloat16)
    earlier = jnp.dot(lower, hot.astype(jnp.bfloat16), preferred_element_type=jnp.float32)
    slot = expert_ids * capacity + jnp.sum(earlier * hot, axis=1).astype(jnp.int32)
    dispatch = (jnp.arange(experts * capacity, dtype=jnp.int32)[:, None] == slot[None, :]).astype(
        jnp.bfloat16
    )
    weight_token = keep.astype(jnp.float32) * gate
    grad_in = cotangent.astype(jnp.float32)
    grad_res = (weight_token[:, None] * grad_in).astype(jnp.bfloat16)
    sent = jnp.dot(
        dispatch,
        jnp.concatenate([rows_two, grad_res], axis=1),
        preferred_element_type=jnp.float32,
    ).astype(jnp.bfloat16)
    sent = sent.reshape(wide_size, local_experts * capacity, 2 * width)
    mine = lax.all_to_all(sent, "wide", split_axis=0, concat_axis=0, tiled=True)
    mine = mine.reshape(wide_size, local_experts, capacity, 2 * width).transpose(1, 0, 2, 3)
    share = wide_size * capacity
    mine = mine.reshape(local_experts * share, 2 * width)
    arrived = gather_rows(mine).reshape(tp_size, local_experts, share, 2 * width)
    arrived = arrived.transpose(1, 0, 2, 3).reshape(local_experts, tp_size * share, 2 * width)
    grad_slots = arrived[:, :, width:]
    arrived = arrived[:, :, :width]
    expert_pre = jnp.einsum("ecd,edf->ecf", arrived, expert_in, preferred_element_type=jnp.float32)
    grad_act = jnp.einsum(
        "ecd,efd->ecf", grad_slots, expert_out, preferred_element_type=jnp.float32
    )
    act_float, gelu_back = jax.vjp(partial(jax.nn.gelu, approximate=True), expert_pre)
    expert_act = act_float.astype(jnp.bfloat16)
    grad_pre = gelu_back(grad_act)[0].astype(jnp.bfloat16)
    expert_terms = jnp.einsum(
        "ecf,efd->ecd", expert_act, expert_out, preferred_element_type=jnp.float32
    ).astype(jnp.bfloat16)
    grad_back_terms = jnp.einsum(
        "ecf,edf->ecd", grad_pre, expert_in, preferred_element_type=jnp.float32
    ).astype(jnp.bfloat16)
    expert_out_grad = jnp.einsum(
        "ecf,ecd->efd", expert_act, grad_slots, preferred_element_type=jnp.float32
    )
    expert_in_grad = jnp.einsum(
        "ecd,ecf->edf", arrived, grad_pre, preferred_element_type=jnp.float32
    )
    terms = jnp.concatenate([expert_terms, grad_back_terms], axis=2)
    terms = terms.reshape(local_experts, tp_size, wide_size, capacity, 2 * width)
    terms = terms.transpose(1, 2, 0, 3, 4).reshape(-1, 2 * width)
    summed = lax.psum_scatter(terms, "tp", scatter_dimension=0, tiled=True)
    summed = summed.reshape(wide_size, local_experts * capacity, 2 * width)
    back = lax.all_to_all(summed, "wide", split_axis=0, concat_axis=0, tiled=True)
    picked = contract_rows(dispatch, back.reshape(experts * capacity, 2 * width))
    returned = picked[:, :width]
    grad_input_expert = picked[:, width:]
    block_out = hidden + weight_token[:, None] * returned
    grad_gate = keep.astype(jnp.float32) * jnp.sum(grad_in * returned, axis=-1)
    grad_logits = ((grad_gate * gate)[:, None] * (hot - probs)).astype(jnp.bfloat16)
    router_full_grad = contract_rows(rows_two, grad_logits)
    grad_normed_two = grad_input_expert + contract_cols(grad_logits, w_router)
    grad_hidden_norm, gain_two_grad = root_norm_back(
        grad_normed_two, normed_two, inverse_two, gain_two
    )
    grad_hidden = grad_in + grad_hidden_norm
    gain_two_all, router_all = lax.psum((gain_two_grad, router_full_grad), ("wide", "tp"))
    grad_rows = gather_rows(grad_hidden.astype(jnp.bfloat16))
    grad_context = jnp.dot(grad_rows, w_out, preferred_element_type=jnp.float32).astype(
        jnp.bfloat16
    )
    out_full_grad = contract_rows(grad_rows, context_low)
    grad_query, grad_key, grad_value, relative_grad = attend_back(
        projected, grad_context, log_totals, relative, local_heads
    )
    grad_joint = jnp.concatenate([grad_query, grad_key, grad_value], axis=1)
    grad_normed_one = sum_rows(contract_cols(grad_joint, w_joint))
    joint_grad = contract_rows(rows_one, grad_joint)
    gain_one_grad = jnp.sum(joint_grad * w_joint.astype(jnp.float32), axis=1) / gain_one
    bias_local = jnp.dot(relative_grad[:local_heads], onehot_table, precision=highest)
    bias_full = lax.dynamic_update_slice_in_dim(
        jnp.zeros(bias_table.shape, jnp.float32), bias_local, lax.axis_index("tp") * local_heads, 0
    )
    gain_one_grad, bias_full, gain_two_all, router_all = lax.optimization_barrier(
        (gain_one_grad, bias_full, gain_two_all, router_all)
    )
    gain_one_all, bias_grad = lax.psum((gain_one_grad, bias_full), ("wide", "tp"))
    grad_x_norm, unused = root_norm_back(grad_normed_one, normed_one, inverse_one, gain_one)
    input_grad = grad_hidden + grad_x_norm
    weight_grads = jnp.concatenate(
        [joint_grad[:, i * BLOCK : i * BLOCK + head_width] for i in range(3)]
        + [out_full_grad[:, :head_width]],
        axis=1,
    ).astype(jnp.bfloat16)
    shard = width // wide_size
    weight_grads = lax.all_to_all(
        weight_grads.reshape(wide_size, shard, 4 * head_width),
        "wide",
        split_axis=0,
        concat_axis=0,
        tiled=True,
    )
    weight_grads = weight_grads.astype(jnp.float32).sum(axis=0)
    query_sum, key_sum, value_sum, out_sum = (
        weight_grads[:, i * head_width : (i + 1) * head_width] for i in range(4)
    )
    first_row = lax.axis_index("wide") * shard
    return (
        block_out,
        input_grad,
        query_sum,
        key_sum,
        value_sum,
        out_sum,
        lax.dynamic_slice_in_dim(gain_one_all, first_row, shard, 0),
        lax.dynamic_slice_in_dim(gain_two_all, first_row, shard, 0),
        lax.dynamic_slice_in_dim(router_all, first_row, shard, 0),
        expert_in_grad,
        expert_out_grad,
        bias_grad,
    )


def solution(mesh):
    placed = (
        P(("wide", "tp"), None),
        P("wide", "tp"),
        P("wide", "tp"),
        P("wide", "tp"),
        P("wide", "tp"),
        P("wide"),
        P("wide"),
        P("wide", None),
        P("wide", None, "tp"),
        P("wide", "tp", None),
        P(),
        P(("wide", "tp"), None),
        P(("wide", "tp")),
        P(("wide", "tp"), None),
    )
    return jax.shard_map(
        per_device,
        mesh=mesh,
        in_specs=placed,
        out_specs=(
            P(("wide", "tp"), None),
            P(("wide", "tp"), None),
            P("wide", "tp"),
            P("wide", "tp"),
            P("wide", "tp"),
            P("wide", "tp"),
            P("wide"),
            P("wide"),
            P("wide", None),
            P("wide", None, "tp"),
            P("wide", "tp", None),
            P(),
        ),
        check_vma=False,
    )
```

```python
from functools import partial

import jax
import jax.numpy as jnp
from jax import lax
from jax.experimental import pallas as pl
from jax.experimental.pallas import tpu as pltpu
from jax.sharding import PartitionSpec as P

HEAD = 64
BUCKETS = 32
LEN = 1024


epsilon = 1e-06
highest = lax.Precision.HIGHEST
bucket_bounds = [12, 16, 23, 32, 46, 64, 91]


BLOCK = 256


def bucket_onehot(length, buckets):
    half = buckets // 2
    exact = half // 2
    offset = jnp.arange(-length, length, dtype=jnp.int32)
    distance = jnp.abs(offset)
    bounds = jnp.asarray(bucket_bounds, dtype=jnp.int32)
    far = exact + jnp.sum(
        (distance[:, None] >= bounds[None, :]).astype(jnp.int32), axis=1, dtype=jnp.int32
    )
    far = jnp.minimum(far, half - 1)
    upper = jnp.where(offset > 0, half, 0).astype(jnp.int32)
    table = upper + jnp.where(distance < exact, distance, far)
    return (table[:, None] == jnp.arange(buckets, dtype=jnp.int32)[None, :]).astype(jnp.float32)


def root_norm(value, gain):
    inverse = lax.rsqrt(jnp.mean(value * value, axis=-1, keepdims=True) + epsilon)
    normed = value * inverse
    return (normed, inverse, normed * gain)


def root_norm_back(grad_in, normed, inverse, gain):
    scaled = grad_in * gain
    inner = jnp.mean(scaled * normed, axis=-1, keepdims=True)
    return (inverse * (scaled - normed * inner), jnp.sum(grad_in * normed, axis=0))


def contract_rows(left, right):
    return lax.dot_general(
        left, right, (((0,), (0,)), ((), ())), preferred_element_type=jnp.float32
    )


def contract_cols(left, right):
    return lax.dot_general(
        left, right, (((1,), (1,)), ((), ())), preferred_element_type=jnp.float32
    )


def gather_rows(rows):
    return lax.all_gather(rows, "tp", axis=0, tiled=True)


def sum_rows(term):
    return lax.psum_scatter(
        term.astype(jnp.bfloat16), "tp", scatter_dimension=0, tiled=True
    ).astype(jnp.float32)


def build_bias(heads, rel_ref, bias_ref):
    for h in range(heads):
        row = jnp.broadcast_to(rel_ref[h : h + 1, :], (BLOCK, 2 * LEN))
        bias_ref[h] = pltpu.roll(row, 0, 1, stride=1, stride_axis=0).T


def flip(value):
    return value.astype(jnp.float32).T.astype(jnp.bfloat16)


def stack_heads(parts):
    pad = jnp.zeros((BLOCK - HEAD * len(parts), parts[0].shape[1]), jnp.float32)
    return jnp.concatenate([*parts, pad], axis=0)


def head_lanes(h, value):
    lane = lax.broadcasted_iota(jnp.int32, value.shape, 1)
    return jnp.where((lane >= h * HEAD) & (lane < (h + 1) * HEAD), value, jnp.zeros_like(value))


def forward_kernel(heads, q_ref, k_ref, v_ref, rel_ref, ctx_ref, lse_ref, bias_ref, vt_ref):
    block = pl.program_id(1)

    @pl.when((pl.program_id(0) == 0) & (block == 0))
    def first():
        build_bias(heads, rel_ref, bias_ref)

    @pl.when(block == 0)
    def new_sequence():
        vt_ref[...] = flip(v_ref[...])

    start = pl.multiple_of(LEN - block * BLOCK, BLOCK)
    parts, logs = ([], [])
    for h in range(heads):
        scores = contract_cols(k_ref[...], head_lanes(h, q_ref[...]))
        scores = scores + bias_ref[h, pl.ds(start, LEN), :]
        top = jnp.max(scores, axis=0, keepdims=True)
        expo = jnp.exp(scores - top)
        total = jnp.sum(expo, axis=0, keepdims=True)
        out = jnp.dot(
            vt_ref[h * HEAD : (h + 1) * HEAD, :],
            expo.astype(jnp.bfloat16),
            preferred_element_type=jnp.float32,
        )
        parts.append(out / total)
        logs.append(top + jnp.log(total))
    ctx_ref[...] = stack_heads(parts).T.astype(jnp.bfloat16)
    logs.append(jnp.zeros((8 - heads, BLOCK), jnp.float32))
    lse_ref[0] = jnp.concatenate(logs, axis=0)


def backward_kernel(
    heads,
    q_ref,
    k_ref,
    v_ref,
    g_ref,
    lse_ref,
    rel_ref,
    dq_ref,
    dk_ref,
    dv_ref,
    drel_ref,
    bias_ref,
    kt_ref,
    sum_ref,
    dk_sum,
    dv_sum,
):
    sequence, block = (pl.program_id(0), pl.program_id(1))
    last = pl.num_programs(1) - 1

    @pl.when((sequence == 0) & (block == 0))
    def first():
        build_bias(heads, rel_ref, bias_ref)
        sum_ref[...] = jnp.zeros_like(sum_ref)

    @pl.when(block == 0)
    def new_sequence():
        kt_ref[...] = flip(k_ref[...])
        dk_sum[...] = jnp.zeros_like(dk_sum)
        dv_sum[...] = jnp.zeros_like(dv_sum)

    start = pl.multiple_of(LEN - block * BLOCK, BLOCK)
    parts = []
    for h in range(heads):
        query = head_lanes(h, q_ref[...])
        grad = head_lanes(h, g_ref[...])
        scores = contract_cols(k_ref[...], query) + bias_ref[h, pl.ds(start, LEN), :]
        weights = jnp.exp(scores - lse_ref[0, h : h + 1, :])
        grad_weights = contract_cols(v_ref[...], grad)
        inner = jnp.sum(weights * grad_weights, axis=0, keepdims=True)
        grad_scores = (weights * (grad_weights - inner)).astype(jnp.bfloat16)
        sum_ref[h, pl.ds(start, LEN), :] += grad_scores.astype(jnp.float32)
        parts.append(
            jnp.dot(
                kt_ref[h * HEAD : (h + 1) * HEAD, :],
                grad_scores,
                preferred_element_type=jnp.float32,
            )
        )
        dk_sum[...] += jnp.dot(grad_scores, query, preferred_element_type=jnp.float32)
        dv_sum[...] += jnp.dot(
            weights.astype(jnp.bfloat16), grad, preferred_element_type=jnp.float32
        )
    dq_ref[...] = stack_heads(parts).T.astype(jnp.bfloat16)

    @pl.when(block == last)
    def end_sequence():
        dk_ref[...] = dk_sum[...].astype(jnp.bfloat16)
        dv_ref[...] = dv_sum[...].astype(jnp.bfloat16)

    @pl.when((sequence == pl.num_programs(0) - 1) & (block == last))
    def end_all():
        drel_ref[...] = jnp.zeros_like(drel_ref)
        for h in range(heads):
            rows = sum_ref[h].T
            count = BLOCK
            while count > 1:
                count //= 2
                rows = rows[:count] + pltpu.roll(rows[count:], 2 * LEN - count, 1)
            drel_ref[h : h + 1, :] = rows


def attention_specs(blocks):
    query = pl.BlockSpec((BLOCK, BLOCK), lambda s, b: (s * blocks + b, 0))
    key = pl.BlockSpec((LEN, BLOCK), lambda s, b: (s, 1))
    value = pl.BlockSpec((LEN, BLOCK), lambda s, b: (s, 2))
    whole = pl.BlockSpec((LEN, BLOCK), lambda s, b: (s, 0))
    rel = pl.BlockSpec((8, 2 * LEN), lambda s, b: (0, 0))
    logs = pl.BlockSpec((1, 8, BLOCK), lambda s, b: (s * blocks + b, 0, 0))
    return (query, key, value, whole, rel, logs)


def attend(projected, relative, heads):
    rows = projected.shape[0]
    blocks = LEN // BLOCK
    query, key, value, whole, rel, logs = attention_specs(blocks)
    return pl.pallas_call(
        partial(forward_kernel, heads),
        grid=(rows // LEN, blocks),
        in_specs=[query, key, value, rel],
        out_specs=[query, logs],
        out_shape=[
            jax.ShapeDtypeStruct((rows, BLOCK), jnp.bfloat16),
            jax.ShapeDtypeStruct((rows // BLOCK, 8, BLOCK), jnp.float32),
        ],
        scratch_shapes=[
            pltpu.VMEM((heads, 2 * LEN, BLOCK), jnp.float32),
            pltpu.VMEM((BLOCK, LEN), jnp.bfloat16),
        ],
        compiler_params=pltpu.CompilerParams(vmem_limit_bytes=48 * 2**20),
        name="attend",
    )(projected, projected, projected, relative)


def attend_back(projected, grad_context, logs_in, relative, heads):
    rows = projected.shape[0]
    blocks = LEN // BLOCK
    query, key, value, whole, rel, logs = attention_specs(blocks)
    return pl.pallas_call(
        partial(backward_kernel, heads),
        grid=(rows // LEN, blocks),
        in_specs=[query, key, value, query, logs, rel],
        out_specs=[query, whole, whole, rel],
        out_shape=[
            jax.ShapeDtypeStruct((rows, BLOCK), jnp.bfloat16),
            jax.ShapeDtypeStruct((rows, BLOCK), jnp.bfloat16),
            jax.ShapeDtypeStruct((rows, BLOCK), jnp.bfloat16),
            jax.ShapeDtypeStruct((8, 2 * LEN), jnp.float32),
        ],
        scratch_shapes=[
            pltpu.VMEM((heads, 2 * LEN, BLOCK), jnp.float32),
            pltpu.VMEM((BLOCK, LEN), jnp.bfloat16),
            pltpu.VMEM((heads, 2 * LEN, BLOCK), jnp.float32),
            pltpu.VMEM((LEN, BLOCK), jnp.float32),
            pltpu.VMEM((LEN, BLOCK), jnp.float32),
        ],
        compiler_params=pltpu.CompilerParams(vmem_limit_bytes=48 * 2**20),
        name="attend_back",
    )(projected, projected, projected, grad_context, logs_in, relative)


def per_device(
    tokens,
    query_weight,
    key_weight,
    value_weight,
    out_weight,
    attn_gain,
    ff_gain,
    router,
    expert_in,
    expert_out,
    bias_table,
    routes,
    keep,
    cotangent,
):
    tp_size = lax.axis_size("tp")
    wide_size = lax.axis_size("wide")
    tok_rows, width = tokens.shape
    local_experts = expert_in.shape[0]
    experts = local_experts * wide_size
    capacity = (5 * tok_rows + 4 * experts - 1) // (4 * experts)
    head_width = query_weight.shape[1]
    local_heads = head_width // HEAD
    tokens_all = gather_rows(tokens)
    packed = jnp.concatenate(
        [
            query_weight,
            key_weight,
            value_weight,
            out_weight,
            router,
            attn_gain[:, None],
            ff_gain[:, None],
        ],
        axis=1,
    )
    packed = lax.all_gather(packed, "wide", axis=0, tiled=True)
    side = ((0, 0), (0, BLOCK - head_width))
    w_query, w_key, w_value, w_out = (
        jnp.pad(packed[:, i * head_width : (i + 1) * head_width], side) for i in range(4)
    )
    w_joint = jnp.concatenate([w_query, w_key, w_value], axis=1)
    at = 4 * head_width
    w_router = packed[:, at : at + experts]
    gain_one = packed[:, at + experts].astype(jnp.float32)
    gain_two = packed[:, at + experts + 1].astype(jnp.float32)
    expert_ids = routes[:, 0]
    hot = (expert_ids[:, None] == jnp.arange(experts, dtype=jnp.int32)[None, :]).astype(jnp.float32)
    lower = (jnp.arange(tok_rows)[:, None] > jnp.arange(tok_rows)[None, :]).astype(jnp.bfloat16)
    earlier = jnp.dot(lower, hot.astype(jnp.bfloat16), preferred_element_type=jnp.float32)
    slot = expert_ids * capacity + jnp.sum(earlier * hot, axis=1).astype(jnp.int32)
    dispatch = (jnp.arange(experts * capacity, dtype=jnp.int32)[:, None] == slot[None, :]).astype(
        jnp.bfloat16
    )

    def to_wide(rows):
        placed = jnp.dot(dispatch, rows, preferred_element_type=jnp.float32).astype(jnp.bfloat16)
        placed = placed.reshape(wide_size, local_experts * capacity, width)
        placed = lax.all_to_all(placed, "wide", split_axis=0, concat_axis=0, tiled=True)
        return placed.reshape(experts * capacity, width)

    def by_expert(rows):
        rows = rows.reshape(tp_size, wide_size, local_experts, capacity, width)
        return rows.transpose(2, 0, 1, 3, 4).reshape(local_experts, -1, width)

    def from_owners(terms):
        terms = terms.astype(jnp.bfloat16)
        terms = terms.reshape(local_experts, tp_size, wide_size, capacity, width)
        terms = terms.transpose(1, 2, 0, 3, 4).reshape(-1, width)
        summed = lax.psum_scatter(terms, "tp", scatter_dimension=0, tiled=True)
        summed = summed.reshape(wide_size, local_experts * capacity, width)
        back = lax.all_to_all(summed, "wide", split_axis=0, concat_axis=0, tiled=True)
        return back.reshape(experts * capacity, width)

    kept = cotangent * keep.astype(jnp.bfloat16)[:, None]
    kept_wide = to_wide(kept)
    onehot_table = bucket_onehot(LEN, BUCKETS)
    table_local = lax.dynamic_slice_in_dim(
        bias_table.astype(jnp.float32), lax.axis_index("tp") * local_heads, local_heads, 0
    )
    relative = jnp.pad(
        lax.dot_general(
            table_local, onehot_table, (((1,), (1,)), ((), ())), precision=highest
        ),
        ((0, 8 - local_heads), (0, 0)),
    )
    tokens_all, kept_wide = lax.optimization_barrier((tokens_all, kept_wide))
    kept_all = gather_rows(kept_wide)
    rows_one = root_norm(tokens_all.astype(jnp.float32), gain_one)[2].astype(jnp.bfloat16)
    x_value = tokens.astype(jnp.float32)
    normed_one, inverse_one, scaled_one = root_norm(x_value, gain_one)
    projected = jnp.dot(rows_one, w_joint, preferred_element_type=jnp.float32).astype(jnp.bfloat16)
    context_low, log_totals = attend(projected, relative, local_heads)
    context_low, kept_all = lax.optimization_barrier((context_low, kept_all))
    attended = sum_rows(contract_cols(context_low, w_out))
    hidden = x_value + attended
    normed_two, inverse_two, scaled_two = root_norm(hidden, gain_two)
    rows_two = scaled_two.astype(jnp.bfloat16)
    logits = jnp.dot(rows_two, w_router, preferred_element_type=jnp.float32)
    probs = jax.nn.softmax(logits, axis=-1)
    gate = jnp.sum(probs * hot, axis=-1)
    weight_token = keep.astype(jnp.float32) * gate
    grad_in = cotangent.astype(jnp.float32)
    arrived = by_expert(gather_rows(to_wide(rows_two)))
    kept_slots = by_expert(kept_all)
    kept_act = jnp.einsum(
        "ecd,efd->ecf", kept_slots, expert_out, preferred_element_type=jnp.float32
    )
    own = lax.axis_index("wide") * local_experts + jnp.arange(local_experts, dtype=jnp.int32)
    own_hot = (own[:, None] == jnp.arange(experts, dtype=jnp.int32)[None, :]).astype(jnp.float32)
    slot_logits = jnp.einsum(
        "ecd,dx->ecx", arrived, w_router, preferred_element_type=jnp.float32
    )
    slot_gate = jnp.sum(
        jax.nn.softmax(slot_logits, axis=-1) * own_hot[:, None, :], axis=-1, keepdims=True
    )
    grad_slots = (slot_gate * kept_slots.astype(jnp.float32)).astype(jnp.bfloat16)
    expert_pre = jnp.einsum("ecd,edf->ecf", arrived, expert_in, preferred_element_type=jnp.float32)
    grad_act = slot_gate * kept_act
    act_float, gelu_back = jax.vjp(partial(jax.nn.gelu, approximate=True), expert_pre)
    expert_act = act_float.astype(jnp.bfloat16)
    grad_pre = gelu_back(grad_act)[0].astype(jnp.bfloat16)
    expert_terms = jnp.einsum(
        "ecf,efd->ecd", expert_act, expert_out, preferred_element_type=jnp.float32
    )
    results = from_owners(expert_terms)
    grad_back_terms = jnp.einsum(
        "ecf,edf->ecd", grad_pre, expert_in, preferred_element_type=jnp.float32
    )
    expert_out_grad = jnp.einsum(
        "ecf,ecd->efd", expert_act, grad_slots, preferred_element_type=jnp.float32
    )
    expert_in_grad = jnp.einsum(
        "ecd,ecf->edf", arrived, grad_pre, preferred_element_type=jnp.float32
    )
    returned = contract_rows(dispatch, results)
    grad_input_expert = contract_rows(dispatch, from_owners(grad_back_terms))
    block_out = hidden + weight_token[:, None] * returned
    grad_gate = keep.astype(jnp.float32) * jnp.sum(grad_in * returned, axis=-1)
    grad_logits = ((grad_gate * gate)[:, None] * (hot - probs)).astype(jnp.bfloat16)
    router_full_grad = contract_rows(rows_two, grad_logits)
    grad_normed_two = grad_input_expert + contract_cols(grad_logits, w_router)
    grad_hidden_norm, gain_two_grad = root_norm_back(
        grad_normed_two, normed_two, inverse_two, gain_two
    )
    grad_hidden = grad_in + grad_hidden_norm
    grad_rows = gather_rows(grad_hidden.astype(jnp.bfloat16))
    grad_rows, expert_in_grad, expert_out_grad = lax.optimization_barrier(
        (grad_rows, expert_in_grad, expert_out_grad)
    )
    grad_context = jnp.dot(grad_rows, w_out, preferred_element_type=jnp.float32).astype(
        jnp.bfloat16
    )
    out_full_grad = contract_rows(grad_rows, context_low)
    grad_query, grad_key, grad_value, relative_grad = attend_back(
        projected, grad_context, log_totals, relative, local_heads
    )
    grad_joint = jnp.concatenate([grad_query, grad_key, grad_value], axis=1)
    input_term = contract_cols(grad_joint, w_joint).astype(jnp.bfloat16)
    joint_grad = contract_rows(rows_one, grad_joint)
    gain_one_grad = jnp.sum(joint_grad * w_joint.astype(jnp.float32), axis=1) / gain_one
    bias_local = jnp.dot(relative_grad[:local_heads], onehot_table, precision=highest)
    shard = width // wide_size
    bias_cols = -(-local_heads * BUCKETS // shard)
    bias_flat = jnp.pad(
        bias_local.reshape(-1), (0, bias_cols * shard - local_heads * BUCKETS)
    ).reshape(shard, bias_cols)
    small = jnp.concatenate(
        [
            router_full_grad,
            gain_two_grad[:, None],
            gain_one_grad[:, None],
            jnp.tile(bias_flat, (wide_size, 1)),
        ],
        axis=1,
    )
    high_part = small.astype(jnp.bfloat16)
    low_part = (small - high_part.astype(jnp.float32)).astype(jnp.bfloat16)
    columns = small.shape[1]
    weight_grads = jnp.concatenate(
        [
            joint_grad[:, i * BLOCK : i * BLOCK + head_width].astype(jnp.bfloat16)
            for i in range(3)
        ]
        + [out_full_grad[:, :head_width].astype(jnp.bfloat16), high_part, low_part],
        axis=1,
    )
    weight_grads, input_term = lax.optimization_barrier((weight_grads, input_term))
    weight_grads = lax.all_to_all(
        weight_grads.reshape(wide_size, shard, 4 * head_width + 2 * columns),
        "wide",
        split_axis=0,
        concat_axis=0,
        tiled=True,
    )
    weight_grads = weight_grads.astype(jnp.float32).sum(axis=0)
    query_sum, key_sum, value_sum, out_sum = (
        weight_grads[:, i * head_width : (i + 1) * head_width] for i in range(4)
    )
    at = 4 * head_width
    small = weight_grads[:, at : at + columns] + weight_grads[:, at + columns :]
    grad_normed_one = sum_rows(input_term)
    grad_normed_one, small = lax.optimization_barrier((grad_normed_one, small))
    grad_x_norm, unused = root_norm_back(grad_normed_one, normed_one, inverse_one, gain_one)
    input_grad = grad_hidden + grad_x_norm
    small_all = lax.all_gather(small, "tp", axis=0, tiled=False)
    bias_grad = small_all[:, :, experts + 2 :].reshape(tp_size, -1)
    bias_grad = bias_grad[:, : local_heads * BUCKETS].reshape(bias_table.shape)
    small = small_all.sum(axis=0)
    return (
        block_out,
        input_grad,
        query_sum,
        key_sum,
        value_sum,
        out_sum,
        small[:, experts + 1],
        small[:, experts],
        small[:, :experts],
        expert_in_grad,
        expert_out_grad,
        bias_grad,
    )


def solution(mesh):
    placed = (
        P(("wide", "tp"), None),
        P("wide", "tp"),
        P("wide", "tp"),
        P("wide", "tp"),
        P("wide", "tp"),
        P("wide"),
        P("wide"),
        P("wide", None),
        P("wide", None, "tp"),
        P("wide", "tp", None),
        P(),
        P(("wide", "tp"), None),
        P(("wide", "tp")),
        P(("wide", "tp"), None),
    )
    return jax.shard_map(
        per_device,
        mesh=mesh,
        in_specs=placed,
        out_specs=(
            P(("wide", "tp"), None),
            P(("wide", "tp"), None),
            P("wide", "tp"),
            P("wide", "tp"),
            P("wide", "tp"),
            P("wide", "tp"),
            P("wide"),
            P("wide"),
            P("wide", None),
            P("wide", None, "tp"),
            P("wide", "tp", None),
            P(),
        ),
        check_vma=False,
    )
```

```python
from functools import partial

import jax
import jax.numpy as jnp
from jax import lax
from jax.experimental import pallas as pl
from jax.experimental.pallas import tpu as pltpu
from jax.sharding import PartitionSpec as P

HEAD = 64
BUCKETS = 32
LEN = 1024


epsilon = 1e-06
highest = lax.Precision.HIGHEST
bucket_bounds = [12, 16, 23, 32, 46, 64, 91]


BLOCK = 256


def bucket_onehot(length, buckets):
    half = buckets // 2
    exact = half // 2
    offset = jnp.arange(-length, length, dtype=jnp.int32)
    distance = jnp.abs(offset)
    bounds = jnp.asarray(bucket_bounds, dtype=jnp.int32)
    far = exact + jnp.sum(
        (distance[:, None] >= bounds[None, :]).astype(jnp.int32), axis=1, dtype=jnp.int32
    )
    far = jnp.minimum(far, half - 1)
    upper = jnp.where(offset > 0, half, 0).astype(jnp.int32)
    table = upper + jnp.where(distance < exact, distance, far)
    return (table[:, None] == jnp.arange(buckets, dtype=jnp.int32)[None, :]).astype(jnp.float32)


def root_norm(value, gain):
    inverse = lax.rsqrt(jnp.mean(value * value, axis=-1, keepdims=True) + epsilon)
    normed = value * inverse
    return (normed, inverse, normed * gain)


def root_norm_back(grad_in, normed, inverse, gain):
    scaled = grad_in * gain
    inner = jnp.mean(scaled * normed, axis=-1, keepdims=True)
    return (inverse * (scaled - normed * inner), jnp.sum(grad_in * normed, axis=0))


def contract_rows(left, right):
    return lax.dot_general(
        left, right, (((0,), (0,)), ((), ())), preferred_element_type=jnp.float32
    )


def contract_cols(left, right):
    return lax.dot_general(
        left, right, (((1,), (1,)), ((), ())), preferred_element_type=jnp.float32
    )


def gather_rows(rows):
    return lax.all_gather(rows, "tp", axis=0, tiled=True)


def sum_rows(term):
    return lax.psum_scatter(
        term.astype(jnp.bfloat16), "tp", scatter_dimension=0, tiled=True
    ).astype(jnp.float32)


def build_bias(heads, rel_ref, bias_ref):
    for h in range(heads):
        row = jnp.broadcast_to(rel_ref[h : h + 1, :], (BLOCK, 2 * LEN))
        bias_ref[h] = pltpu.roll(row, 0, 1, stride=1, stride_axis=0).T


def flip(value):
    return value.astype(jnp.float32).T.astype(jnp.bfloat16)


def stack_heads(parts):
    pad = jnp.zeros((BLOCK - HEAD * len(parts), parts[0].shape[1]), jnp.float32)
    return jnp.concatenate([*parts, pad], axis=0)


def head_lanes(h, value):
    lane = lax.broadcasted_iota(jnp.int32, value.shape, 1)
    return jnp.where((lane >= h * HEAD) & (lane < (h + 1) * HEAD), value, jnp.zeros_like(value))


def forward_kernel(heads, q_ref, k_ref, v_ref, rel_ref, ctx_ref, lse_ref, bias_ref, vt_ref):
    block = pl.program_id(1)

    @pl.when((pl.program_id(0) == 0) & (block == 0))
    def first():
        build_bias(heads, rel_ref, bias_ref)

    @pl.when(block == 0)
    def new_sequence():
        vt_ref[...] = flip(v_ref[...])

    start = pl.multiple_of(LEN - block * BLOCK, BLOCK)
    parts, logs = ([], [])
    for h in range(heads):
        scores = contract_cols(k_ref[...], head_lanes(h, q_ref[...]))
        scores = scores + bias_ref[h, pl.ds(start, LEN), :]
        top = jnp.max(scores, axis=0, keepdims=True)
        expo = jnp.exp(scores - top)
        total = jnp.sum(expo, axis=0, keepdims=True)
        out = jnp.dot(
            vt_ref[h * HEAD : (h + 1) * HEAD, :],
            expo.astype(jnp.bfloat16),
            preferred_element_type=jnp.float32,
        )
        parts.append(out / total)
        logs.append(top + jnp.log(total))
    ctx_ref[...] = stack_heads(parts).T.astype(jnp.bfloat16)
    logs.append(jnp.zeros((8 - heads, BLOCK), jnp.float32))
    lse_ref[0] = jnp.concatenate(logs, axis=0)


def backward_kernel(
    heads,
    q_ref,
    k_ref,
    v_ref,
    g_ref,
    lse_ref,
    rel_ref,
    dq_ref,
    dk_ref,
    dv_ref,
    drel_ref,
    bias_ref,
    kt_ref,
    sum_ref,
    dk_sum,
    dv_sum,
):
    sequence, block = (pl.program_id(0), pl.program_id(1))
    last = pl.num_programs(1) - 1

    @pl.when((sequence == 0) & (block == 0))
    def first():
        build_bias(heads, rel_ref, bias_ref)
        sum_ref[...] = jnp.zeros_like(sum_ref)

    @pl.when(block == 0)
    def new_sequence():
        kt_ref[...] = flip(k_ref[...])
        dk_sum[...] = jnp.zeros_like(dk_sum)
        dv_sum[...] = jnp.zeros_like(dv_sum)

    start = pl.multiple_of(LEN - block * BLOCK, BLOCK)
    parts = []
    for h in range(heads):
        query = head_lanes(h, q_ref[...])
        grad = head_lanes(h, g_ref[...])
        scores = contract_cols(k_ref[...], query) + bias_ref[h, pl.ds(start, LEN), :]
        weights = jnp.exp(scores - lse_ref[0, h : h + 1, :])
        grad_weights = contract_cols(v_ref[...], grad)
        inner = jnp.sum(weights * grad_weights, axis=0, keepdims=True)
        grad_scores = (weights * (grad_weights - inner)).astype(jnp.bfloat16)
        sum_ref[h, pl.ds(start, LEN), :] += grad_scores.astype(jnp.float32)
        parts.append(
            jnp.dot(
                kt_ref[h * HEAD : (h + 1) * HEAD, :],
                grad_scores,
                preferred_element_type=jnp.float32,
            )
        )
        dk_sum[...] += jnp.dot(grad_scores, query, preferred_element_type=jnp.float32)
        dv_sum[...] += jnp.dot(
            weights.astype(jnp.bfloat16), grad, preferred_element_type=jnp.float32
        )
    dq_ref[...] = stack_heads(parts).T.astype(jnp.bfloat16)

    @pl.when(block == last)
    def end_sequence():
        dk_ref[...] = dk_sum[...].astype(jnp.bfloat16)
        dv_ref[...] = dv_sum[...].astype(jnp.bfloat16)

    @pl.when((sequence == pl.num_programs(0) - 1) & (block == last))
    def end_all():
        drel_ref[...] = jnp.zeros_like(drel_ref)
        for h in range(heads):
            rows = sum_ref[h].T
            count = BLOCK
            while count > 1:
                count //= 2
                rows = rows[:count] + pltpu.roll(rows[count:], 2 * LEN - count, 1)
            drel_ref[h : h + 1, :] = rows


def attention_specs(blocks):
    query = pl.BlockSpec((BLOCK, BLOCK), lambda s, b: (s * blocks + b, 0))
    key = pl.BlockSpec((LEN, BLOCK), lambda s, b: (s, 1))
    value = pl.BlockSpec((LEN, BLOCK), lambda s, b: (s, 2))
    whole = pl.BlockSpec((LEN, BLOCK), lambda s, b: (s, 0))
    rel = pl.BlockSpec((8, 2 * LEN), lambda s, b: (0, 0))
    logs = pl.BlockSpec((1, 8, BLOCK), lambda s, b: (s * blocks + b, 0, 0))
    return (query, key, value, whole, rel, logs)


def attend(projected, relative, heads):
    rows = projected.shape[0]
    blocks = LEN // BLOCK
    query, key, value, whole, rel, logs = attention_specs(blocks)
    return pl.pallas_call(
        partial(forward_kernel, heads),
        grid=(rows // LEN, blocks),
        in_specs=[query, key, value, rel],
        out_specs=[query, logs],
        out_shape=[
            jax.ShapeDtypeStruct((rows, BLOCK), jnp.bfloat16),
            jax.ShapeDtypeStruct((rows // BLOCK, 8, BLOCK), jnp.float32),
        ],
        scratch_shapes=[
            pltpu.VMEM((heads, 2 * LEN, BLOCK), jnp.float32),
            pltpu.VMEM((BLOCK, LEN), jnp.bfloat16),
        ],
        compiler_params=pltpu.CompilerParams(vmem_limit_bytes=48 * 2**20),
        name="attend",
    )(projected, projected, projected, relative)


def attend_back(projected, grad_context, logs_in, relative, heads):
    rows = projected.shape[0]
    blocks = LEN // BLOCK
    query, key, value, whole, rel, logs = attention_specs(blocks)
    return pl.pallas_call(
        partial(backward_kernel, heads),
        grid=(rows // LEN, blocks),
        in_specs=[query, key, value, query, logs, rel],
        out_specs=[query, whole, whole, rel],
        out_shape=[
            jax.ShapeDtypeStruct((rows, BLOCK), jnp.bfloat16),
            jax.ShapeDtypeStruct((rows, BLOCK), jnp.bfloat16),
            jax.ShapeDtypeStruct((rows, BLOCK), jnp.bfloat16),
            jax.ShapeDtypeStruct((8, 2 * LEN), jnp.float32),
        ],
        scratch_shapes=[
            pltpu.VMEM((heads, 2 * LEN, BLOCK), jnp.float32),
            pltpu.VMEM((BLOCK, LEN), jnp.bfloat16),
            pltpu.VMEM((heads, 2 * LEN, BLOCK), jnp.float32),
            pltpu.VMEM((LEN, BLOCK), jnp.float32),
            pltpu.VMEM((LEN, BLOCK), jnp.float32),
        ],
        compiler_params=pltpu.CompilerParams(vmem_limit_bytes=48 * 2**20),
        name="attend_back",
    )(projected, projected, projected, grad_context, logs_in, relative)


def per_device(
    tokens,
    query_weight,
    key_weight,
    value_weight,
    out_weight,
    attn_gain,
    ff_gain,
    router,
    expert_in,
    expert_out,
    bias_table,
    routes,
    keep,
    cotangent,
):
    tp_size = lax.axis_size("tp")
    wide_size = lax.axis_size("wide")
    tok_rows, width = tokens.shape
    local_experts = expert_in.shape[0]
    experts = local_experts * wide_size
    capacity = (5 * tok_rows + 4 * experts - 1) // (4 * experts)
    head_width = query_weight.shape[1]
    local_heads = head_width // HEAD
    packed = jnp.concatenate(
        [
            query_weight,
            key_weight,
            value_weight,
            out_weight,
            router,
            attn_gain[:, None],
            ff_gain[:, None],
        ],
        axis=1,
    )
    packed = lax.all_gather(packed, "wide", axis=0, tiled=True)
    kept = cotangent * keep.astype(jnp.bfloat16)[:, None]
    packed, kept, tokens = lax.optimization_barrier((packed, kept, tokens))
    tokens_all = gather_rows(tokens)
    side = ((0, 0), (0, BLOCK - head_width))
    w_query, w_key, w_value, w_out = (
        jnp.pad(packed[:, i * head_width : (i + 1) * head_width], side) for i in range(4)
    )
    w_joint = jnp.concatenate([w_query, w_key, w_value], axis=1)
    at = 4 * head_width
    w_router = packed[:, at : at + experts]
    gain_one = packed[:, at + experts].astype(jnp.float32)
    gain_two = packed[:, at + experts + 1].astype(jnp.float32)
    expert_ids = routes[:, 0]
    hot = (expert_ids[:, None] == jnp.arange(experts, dtype=jnp.int32)[None, :]).astype(jnp.float32)
    lower = (jnp.arange(tok_rows)[:, None] > jnp.arange(tok_rows)[None, :]).astype(jnp.bfloat16)
    earlier = jnp.dot(lower, hot.astype(jnp.bfloat16), preferred_element_type=jnp.float32)
    slot = expert_ids * capacity + jnp.sum(earlier * hot, axis=1).astype(jnp.int32)
    dispatch = (jnp.arange(experts * capacity, dtype=jnp.int32)[:, None] == slot[None, :]).astype(
        jnp.bfloat16
    )

    def to_wide(rows):
        placed = jnp.dot(dispatch, rows, preferred_element_type=jnp.float32).astype(jnp.bfloat16)
        placed = placed.reshape(wide_size, local_experts * capacity, width)
        placed = lax.all_to_all(placed, "wide", split_axis=0, concat_axis=0, tiled=True)
        return placed.reshape(experts * capacity, width)

    def by_expert(rows):
        rows = rows.reshape(tp_size, wide_size, local_experts, capacity, width)
        return rows.transpose(2, 0, 1, 3, 4).reshape(local_experts, -1, width)

    def from_owners(terms):
        terms = terms.astype(jnp.bfloat16)
        terms = terms.reshape(local_experts, tp_size, wide_size, capacity, width)
        terms = terms.transpose(1, 2, 0, 3, 4).reshape(-1, width)
        summed = lax.psum_scatter(terms, "tp", scatter_dimension=0, tiled=True)
        summed = summed.reshape(wide_size, local_experts * capacity, width)
        back = lax.all_to_all(summed, "wide", split_axis=0, concat_axis=0, tiled=True)
        return back.reshape(experts * capacity, width)

    kept_wide = to_wide(kept)
    onehot_table = bucket_onehot(LEN, BUCKETS)
    table_local = lax.dynamic_slice_in_dim(
        bias_table.astype(jnp.float32), lax.axis_index("tp") * local_heads, local_heads, 0
    )
    relative = jnp.pad(
        lax.dot_general(
            table_local, onehot_table, (((1,), (1,)), ((), ())), precision=highest
        ),
        ((0, 8 - local_heads), (0, 0)),
    )
    tokens_all, kept_wide = lax.optimization_barrier((tokens_all, kept_wide))
    kept_all = gather_rows(kept_wide)
    rows_one = root_norm(tokens_all.astype(jnp.float32), gain_one)[2].astype(jnp.bfloat16)
    x_value = tokens.astype(jnp.float32)
    normed_one, inverse_one, scaled_one = root_norm(x_value, gain_one)
    projected = jnp.dot(rows_one, w_joint, preferred_element_type=jnp.float32).astype(jnp.bfloat16)
    context_low, log_totals = attend(projected, relative, local_heads)
    context_low, kept_all = lax.optimization_barrier((context_low, kept_all))
    attended = sum_rows(contract_cols(context_low, w_out))
    hidden = x_value + attended
    normed_two, inverse_two, scaled_two = root_norm(hidden, gain_two)
    rows_two = scaled_two.astype(jnp.bfloat16)
    logits = jnp.dot(rows_two, w_router, preferred_element_type=jnp.float32)
    probs = jax.nn.softmax(logits, axis=-1)
    gate = jnp.sum(probs * hot, axis=-1)
    weight_token = keep.astype(jnp.float32) * gate
    grad_in = cotangent.astype(jnp.float32)
    arrived = by_expert(gather_rows(to_wide(rows_two)))
    kept_slots = by_expert(kept_all)
    kept_act = jnp.einsum(
        "ecd,efd->ecf", kept_slots, expert_out, preferred_element_type=jnp.float32
    )
    own = lax.axis_index("wide") * local_experts + jnp.arange(local_experts, dtype=jnp.int32)
    own_hot = (own[:, None] == jnp.arange(experts, dtype=jnp.int32)[None, :]).astype(jnp.float32)
    slot_logits = jnp.einsum(
        "ecd,dx->ecx", arrived, w_router, preferred_element_type=jnp.float32
    )
    slot_gate = jnp.sum(
        jax.nn.softmax(slot_logits, axis=-1) * own_hot[:, None, :], axis=-1, keepdims=True
    )
    grad_slots = (slot_gate * kept_slots.astype(jnp.float32)).astype(jnp.bfloat16)
    expert_pre = jnp.einsum("ecd,edf->ecf", arrived, expert_in, preferred_element_type=jnp.float32)
    grad_act = slot_gate * kept_act
    act_float, gelu_back = jax.vjp(partial(jax.nn.gelu, approximate=True), expert_pre)
    expert_act = act_float.astype(jnp.bfloat16)
    grad_pre = gelu_back(grad_act)[0].astype(jnp.bfloat16)
    expert_terms = jnp.einsum(
        "ecf,efd->ecd", expert_act, expert_out, preferred_element_type=jnp.float32
    )
    results = from_owners(expert_terms)
    grad_back_terms = jnp.einsum(
        "ecf,edf->ecd", grad_pre, expert_in, preferred_element_type=jnp.float32
    )
    expert_out_grad = jnp.einsum(
        "ecf,ecd->efd", expert_act, grad_slots, preferred_element_type=jnp.float32
    )
    expert_in_grad = jnp.einsum(
        "ecd,ecf->edf", arrived, grad_pre, preferred_element_type=jnp.float32
    )
    returned = contract_rows(dispatch, results)
    grad_input_expert = contract_rows(dispatch, from_owners(grad_back_terms))
    block_out = hidden + weight_token[:, None] * returned
    grad_gate = keep.astype(jnp.float32) * jnp.sum(grad_in * returned, axis=-1)
    grad_logits = ((grad_gate * gate)[:, None] * (hot - probs)).astype(jnp.bfloat16)
    router_full_grad = contract_rows(rows_two, grad_logits)
    grad_normed_two = grad_input_expert + contract_cols(grad_logits, w_router)
    grad_hidden_norm, gain_two_grad = root_norm_back(
        grad_normed_two, normed_two, inverse_two, gain_two
    )
    grad_hidden = grad_in + grad_hidden_norm
    grad_rows = gather_rows(grad_hidden.astype(jnp.bfloat16))
    grad_rows, expert_in_grad, expert_out_grad = lax.optimization_barrier(
        (grad_rows, expert_in_grad, expert_out_grad)
    )
    grad_context = jnp.dot(grad_rows, w_out, preferred_element_type=jnp.float32).astype(
        jnp.bfloat16
    )
    out_full_grad = contract_rows(grad_rows, context_low)
    grad_query, grad_key, grad_value, relative_grad = attend_back(
        projected, grad_context, log_totals, relative, local_heads
    )
    grad_joint = jnp.concatenate([grad_query, grad_key, grad_value], axis=1)
    input_term = contract_cols(grad_joint, w_joint).astype(jnp.bfloat16)
    joint_grad = contract_rows(rows_one, grad_joint)
    gain_one_grad = jnp.sum(joint_grad * w_joint.astype(jnp.float32), axis=1) / gain_one
    bias_local = jnp.dot(relative_grad[:local_heads], onehot_table, precision=highest)
    shard = width // wide_size
    bias_cols = -(-local_heads * BUCKETS // shard)
    bias_flat = jnp.pad(
        bias_local.reshape(-1), (0, bias_cols * shard - local_heads * BUCKETS)
    ).reshape(shard, bias_cols)
    small = jnp.concatenate(
        [
            router_full_grad,
            gain_two_grad[:, None],
            gain_one_grad[:, None],
            jnp.tile(bias_flat, (wide_size, 1)),
        ],
        axis=1,
    )
    high_part = small.astype(jnp.bfloat16)
    low_part = (small - high_part.astype(jnp.float32)).astype(jnp.bfloat16)
    columns = small.shape[1]
    weight_grads = jnp.concatenate(
        [
            joint_grad[:, i * BLOCK : i * BLOCK + head_width].astype(jnp.bfloat16)
            for i in range(3)
        ]
        + [out_full_grad[:, :head_width].astype(jnp.bfloat16), high_part, low_part],
        axis=1,
    )
    weight_grads, input_term = lax.optimization_barrier((weight_grads, input_term))
    weight_grads = lax.all_to_all(
        weight_grads.reshape(wide_size, shard, 4 * head_width + 2 * columns),
        "wide",
        split_axis=0,
        concat_axis=0,
        tiled=True,
    )
    weight_grads = weight_grads.astype(jnp.float32).sum(axis=0)
    query_sum, key_sum, value_sum, out_sum = (
        weight_grads[:, i * head_width : (i + 1) * head_width] for i in range(4)
    )
    at = 4 * head_width
    small = weight_grads[:, at : at + columns] + weight_grads[:, at + columns :]
    grad_normed_one = sum_rows(input_term)
    grad_normed_one, small = lax.optimization_barrier((grad_normed_one, small))
    grad_x_norm, unused = root_norm_back(grad_normed_one, normed_one, inverse_one, gain_one)
    input_grad = grad_hidden + grad_x_norm
    small_all = lax.all_gather(small, "tp", axis=0, tiled=False)
    bias_grad = small_all[:, :, experts + 2 :].reshape(tp_size, -1)
    bias_grad = bias_grad[:, : local_heads * BUCKETS].reshape(bias_table.shape)
    small = small_all.sum(axis=0)
    return (
        block_out,
        input_grad,
        query_sum,
        key_sum,
        value_sum,
        out_sum,
        small[:, experts + 1],
        small[:, experts],
        small[:, :experts],
        expert_in_grad,
        expert_out_grad,
        bias_grad,
    )


def solution(mesh):
    placed = (
        P(("wide", "tp"), None),
        P("wide", "tp"),
        P("wide", "tp"),
        P("wide", "tp"),
        P("wide", "tp"),
        P("wide"),
        P("wide"),
        P("wide", None),
        P("wide", None, "tp"),
        P("wide", "tp", None),
        P(),
        P(("wide", "tp"), None),
        P(("wide", "tp")),
        P(("wide", "tp"), None),
    )
    return jax.shard_map(
        per_device,
        mesh=mesh,
        in_specs=placed,
        out_specs=(
            P(("wide", "tp"), None),
            P(("wide", "tp"), None),
            P("wide", "tp"),
            P("wide", "tp"),
            P("wide", "tp"),
            P("wide", "tp"),
            P("wide"),
            P("wide"),
            P("wide", None),
            P("wide", None, "tp"),
            P("wide", "tp", None),
            P(),
        ),
        check_vma=False,
    )
```
